32 devices in a mesh: grp: 2 (over y), blk: 16 (over z, x, core).
Axes of the slice: x: 2, y: 2, z: 4, core: 2. Of those that a mesh axis runs over, the one named last changes fastest.
Arguments:
- tokens: bfloat16 [64, 8192], P(('grp', 'blk')), parts along dimension 0, may hold values from -6 to 6
- gate_matrix: bfloat16 [8192, 16384], P(None, 'blk'), may hold values from -0.0625 to 0.0625
- up_matrix: bfloat16 [8192, 16384], P(None, 'blk'), may hold values from -0.0625 to 0.0625
- down_matrix: bfloat16 [16384, 8192], P('blk'), may hold values from -0.046875 to 0.046875
- gate_adapter_input: bfloat16 [8192, 16], replicated, may hold values from -0.0625 to 0.0625
- gate_adapter_output: bfloat16 [16, 16384], P(None, 'blk'), may hold values from -1.5 to 1.5
- up_adapter_input: bfloat16 [8192, 16], replicated, may hold values from -0.0625 to 0.0625
- up_adapter_output: bfloat16 [16, 16384], P(None, 'blk'), may hold values from -1.5 to 1.5
- down_adapter_input: bfloat16 [16384, 16], P('blk'), may hold values from -0.046875 to 0.046875
- down_adapter_output: bfloat16 [16, 8192], replicated, may hold values from -1.5 to 1.5
Outputs:
- mixed: bfloat16 [64, 8192], P(('grp', 'blk')), parts along dimension 0
- importance: float32 [64], P(('grp', 'blk')), parts along dimension 0
The draws below stay inside these ranges and needn't reach their ends.
There are 2 independent parts, one for each index of `grp`. The reference program is written for one: setup_inputs(seed, part) draws one part's arguments, and reference() takes and returns one part's arrays. A program takes and returns all parts, laid end to end along the dimension named above; an argument that names none is the same for every part. Nothing has to cross between parts.
All inputs are finite; a program needn't handle non-finite values.
Results may differ from the reference program's by a relative error of at most 0.0054.
Values may be sent and summed in bfloat16 or wider, within the bound.
No kernel may reach another device: no remote copies, remote signals or barrier semaphores. Data moves between devices by JAX's collectives and lax.ppermute only.
A program may use at most 128 MiB of HBM per device.

```python
import jax
import jax.numpy as jnp
from jax import lax

MODEL_WIDTH = 8192
HIDDEN_UNITS = 16384
ADAPTER_RANK = 16
TOKENS = 32


def shard_levels(stream_key, shape, cuts, low, top_value):
    gain, own = 1.0, jax.random.fold_in(stream_key, 6)
    for dim, shards_of in cuts:
        steps = jnp.exp(jax.random.uniform(jax.random.fold_in(own, dim), (shards_of,), jnp.float32, low / len(cuts), top_value / len(cuts)))
        gain = gain * jnp.repeat(steps, shape[dim] // shards_of).reshape([-1 if axis == dim else 1 for axis in range(len(shape))])
    return gain


def normal_values(key, extent, scale, bound, pieces=(), held_as=jnp.bfloat16):
    factor_of = shard_levels(key, extent, pieces, -0.22, 0.18) if pieces else 1.0
    array = jax.random.normal(key, extent, jnp.float32) * scale * factor_of
    return jnp.minimum(jnp.maximum(array, -bound), bound).astype(held_as)


def setup_inputs(seed: int = 0, part: int = 0) -> dict:
    keys = jax.random.split(jax.random.key(seed), 11)
    part_keys = jax.random.split(jax.random.fold_in(keys[10], part), 11)
    tokens = normal_values(part_keys[0], (TOKENS, MODEL_WIDTH), 1.0, 6.0, ((0, 16),))
    gate_matrix = normal_values(keys[1], (MODEL_WIDTH, HIDDEN_UNITS), MODEL_WIDTH ** -0.5, 0.0625, ((1, 16),))
    up_matrix = normal_values(keys[2], (MODEL_WIDTH, HIDDEN_UNITS), MODEL_WIDTH ** -0.5, 0.0625, ((1, 16),))
    down_matrix = normal_values(keys[3], (HIDDEN_UNITS, MODEL_WIDTH), HIDDEN_UNITS ** -0.5, 0.046875, ((0, 16),))
    gate_adapter_input = normal_values(keys[4], (MODEL_WIDTH, ADAPTER_RANK), MODEL_WIDTH ** -0.5, 0.0625)
    gate_adapter_output = normal_values(keys[5], (ADAPTER_RANK, HIDDEN_UNITS), ADAPTER_RANK ** -0.5, 1.5, ((1, 16),))
    up_adapter_input = normal_values(keys[6], (MODEL_WIDTH, ADAPTER_RANK), MODEL_WIDTH ** -0.5, 0.0625)
    up_adapter_output = normal_values(keys[7], (ADAPTER_RANK, HIDDEN_UNITS), ADAPTER_RANK ** -0.5, 1.5, ((1, 16),))
    down_adapter_input = normal_values(keys[8], (HIDDEN_UNITS, ADAPTER_RANK), HIDDEN_UNITS ** -0.5, 0.046875, ((0, 16),))
    down_adapter_output = normal_values(keys[9], (ADAPTER_RANK, MODEL_WIDTH), ADAPTER_RANK ** -0.5, 1.5)
    return {"tokens": tokens, "gate_matrix": gate_matrix, "up_matrix": up_matrix, "down_matrix": down_matrix, "gate_adapter_input": gate_adapter_input, "gate_adapter_output": gate_adapter_output, "up_adapter_input": up_adapter_input, "up_adapter_output": up_adapter_output, "down_adapter_input": down_adapter_input, "down_adapter_output": down_adapter_output}


def reference(tokens, gate_matrix, up_matrix, down_matrix, gate_adapter_input, gate_adapter_output, up_adapter_input, up_adapter_output, down_adapter_input, down_adapter_output):
    gate_reduced = jnp.dot(tokens, gate_adapter_input, preferred_element_type=jnp.float32).astype(jnp.bfloat16)
    up_reduced = jnp.dot(tokens, up_adapter_input, preferred_element_type=jnp.float32).astype(jnp.bfloat16)
    gate_value = jnp.dot(tokens, gate_matrix, preferred_element_type=jnp.float32) + 0.5 * jnp.dot(gate_reduced, gate_adapter_output, preferred_element_type=jnp.float32)
    up_value = jnp.dot(tokens, up_matrix, preferred_element_type=jnp.float32) + 0.5 * jnp.dot(up_reduced, up_adapter_output, preferred_element_type=jnp.float32)
    hidden_state = (jax.nn.silu(gate_value) * up_value).astype(jnp.bfloat16)
    base = jnp.dot(hidden_state, down_matrix, preferred_element_type=jnp.float32)
    middle_state = jnp.dot(hidden_state, down_adapter_input, preferred_element_type=jnp.float32)
    adapter_branch = 0.5 * jnp.dot(middle_state, down_adapter_output.astype(jnp.float32), precision=lax.Precision.HIGHEST)
    mixed = (base + adapter_branch).astype(jnp.bfloat16)
    importance = jnp.sqrt(lax.optimization_barrier(jnp.sum(adapter_branch * adapter_branch, axis=-1)))
    return (mixed, importance)
```

```python
import functools

import jax
import jax.numpy as jnp
from jax import lax
from jax.experimental import pallas as pl
from jax.experimental.pallas import tpu as pltpu
from jax.sharding import PartitionSpec as P

MIB = 1 << 20


def swap(value, size, bit):
    return lax.ppermute(value, "blk", [(i, i ^ bit) for i in range(size)])


def hidden_kernel(rows, gate, up, gate_in, gate_out, up_in, up_out, hidden):
    x = rows[...]
    dims = (((1,), (1,)), ((), ()))
    gate_low = lax.dot_general(x, gate_in[...], dims, preferred_element_type=jnp.float32)
    up_low = lax.dot_general(x, up_in[...], dims, preferred_element_type=jnp.float32)
    gate_low = gate_low.astype(jnp.bfloat16)
    up_low = up_low.astype(jnp.bfloat16)
    width = hidden.shape[1]
    step = 256

    @pl.loop(0, width // step)
    def _(j):
        cols = pl.ds(pl.multiple_of(j * step, step), step)
        g = jnp.dot(x, gate[:, cols], preferred_element_type=jnp.float32)
        g += 0.5 * jnp.dot(gate_low, gate_out[:, cols], preferred_element_type=jnp.float32)
        u = jnp.dot(x, up[:, cols], preferred_element_type=jnp.float32)
        u += 0.5 * jnp.dot(up_low, up_out[:, cols], preferred_element_type=jnp.float32)
        hidden[:, cols] = (g / (1.0 + jnp.exp(-g)) * u).astype(jnp.bfloat16)


def down_kernel(hidden, down, down_in, base, middle):
    h = hidden[...]
    dims = (((1,), (1,)), ((), ()))
    middle[...] = lax.dot_general(h, down_in[...], dims, preferred_element_type=jnp.float32)
    step = 512

    @pl.loop(0, base.shape[1] // step)
    def _(j):
        cols = pl.ds(pl.multiple_of(j * step, step), step)
        base[:, cols] = jnp.dot(h, down[:, cols], preferred_element_type=jnp.float32).astype(jnp.bfloat16)


def body(size, tokens, gate, up, down, gate_in, gate_out, up_in, up_out, down_in, down_out):
    bits = [1 << b for b in range(size.bit_length() - 1)]
    rows = tokens
    for bit in reversed(bits):
        rows = jnp.concatenate([rows, swap(rows, size, bit)], axis=0)
    vmem = functools.partial(pltpu.with_memory_space_constraint, memory_space=pltpu.VMEM)
    whole = pl.BlockSpec(memory_space=pltpu.VMEM)
    count, width = rows.shape[0], gate.shape[1]
    hidden = pl.pallas_call(
        hidden_kernel,
        out_shape=jax.ShapeDtypeStruct((count, width), jnp.bfloat16),
        in_specs=[whole] * 7,
        out_specs=whole,
        compiler_params=pltpu.CompilerParams(vmem_limit_bytes=8 * MIB),
        name="hidden",
    )(rows, vmem(gate), vmem(up), gate_in.T, gate_out, up_in.T, up_out)
    base, middle = pl.pallas_call(
        down_kernel,
        out_shape=[
            jax.ShapeDtypeStruct((count, down.shape[1]), jnp.bfloat16),
            jax.ShapeDtypeStruct((count, down_in.shape[1]), jnp.float32),
        ],
        in_specs=[whole] * 3,
        out_specs=[whole] * 2,
        compiler_params=pltpu.CompilerParams(vmem_limit_bytes=8 * MIB),
        name="down",
    )(hidden, vmem(down), down_in.T)
    for bit in bits:
        half = base.shape[0] // 2
        got_base = swap(base[half:], size, bit)
        got_middle = swap(middle[half:], size, bit)
        base = base[:half].astype(jnp.float32) + got_base.astype(jnp.float32)
        middle = middle[:half] + got_middle
        if half > tokens.shape[0]:
            base = base.astype(jnp.bfloat16)
    adapter = 0.5 * jnp.dot(middle, down_out.astype(jnp.float32), precision=lax.Precision.HIGHEST)
    mixed = (base + adapter).astype(jnp.bfloat16)
    importance = jnp.sqrt(jnp.sum(adapter * adapter, axis=-1))
    return mixed, importance


def solution(mesh):
    size = mesh.shape["blk"]
    in_specs = (
        P(("grp", "blk"), None),
        P(None, "blk"),
        P(None, "blk"),
        P("blk", None),
        P(),
        P(None, "blk"),
        P(),
        P(None, "blk"),
        P("blk", None),
        P(),
    )
    out_specs = (P(("grp", "blk"), None), P(("grp", "blk")))
    return jax.shard_map(
        functools.partial(body, size), mesh=mesh, in_specs=in_specs, out_specs=out_specs, check_vma=False
    )
```

```python
import functools

import jax
import jax.numpy as jnp
from jax import lax
from jax.experimental import pallas as pl
from jax.experimental.pallas import tpu as pltpu
from jax.sharding import PartitionSpec as P

MIB = 1 << 20
LANES = 128
PIECES = 4
FLOPS_PER_US = 10**9
HOLD_US, MERGE_US = 1, (3, 6, 2)
F32, BF16 = jnp.float32, jnp.bfloat16
WHOLE = pl.BlockSpec(memory_space=pltpu.VMEM)
FAR = pl.BlockSpec(memory_space=pltpu.HBM)
vmem = functools.partial(pltpu.with_memory_space_constraint, memory_space=pltpu.VMEM)
hbm = functools.partial(pltpu.with_memory_space_constraint, memory_space=pltpu.HBM)


def call(kernel, out_shape, in_specs, us, name, limit=2 * MIB, scratch=()):
    many = isinstance(out_shape, list)
    return pl.pallas_call(
        kernel,
        out_shape=out_shape,
        in_specs=in_specs,
        out_specs=[WHOLE] * len(out_shape) if many else WHOLE,
        scratch_shapes=list(scratch),
        compiler_params=pltpu.CompilerParams(vmem_limit_bytes=limit),
        cost_estimate=pl.CostEstimate(flops=int(us * FLOPS_PER_US), bytes_accessed=0, transcendentals=0),
        name=name,
    )


def rounds_of(size, along_x):
    masks = [1 << b for b in range(size.bit_length() - 1)]
    x, z = 2, 2 * along_x
    return [[m] for m in reversed(masks) if m not in (1, x, z)] + [[x, z, x ^ z], [1]]


def swap(value, size, mask):
    return lax.ppermute(value, "blk", [(i, i ^ mask) for i in range(size)])


def hold_kernel(source, target):
    pltpu.sync_copy(source, target)


def merge_kernel(*refs):
    merged = refs[-1]
    count = refs[0].shape[0]
    for i, part in enumerate(refs[:-1]):
        merged[i * count : (i + 1) * count] = part[...]


def merge(parts, us):
    count, width = parts[0].shape
    shape = jax.ShapeDtypeStruct((len(parts) * count, width), parts[0].dtype)
    return call(merge_kernel, shape, [WHOLE] * len(parts), us, "merge")(*parts)


def put(sums, middle, targets):
    high = middle.astype(BF16)
    low = (middle - high.astype(F32)).astype(BF16)
    width, rank = sums.shape[1], middle.shape[1]
    count = targets[0].shape[0]
    for i, target in enumerate(targets):
        rows = slice(i * count, (i + 1) * count)
        target[:, :width] = sums[rows].astype(BF16)
        target[:, width : width + rank] = high[rows]
        target[:, width + LANES : width + LANES + rank] = low[rows]


def take(parts):
    width = parts[0].shape[1] - 2 * LANES
    sums = sum(part[:, :width].astype(F32) for part in parts)
    middle = sum(part[:, width : width + LANES].astype(F32) + part[:, width + LANES :].astype(F32) for part in parts)
    return sums, middle


def add_kernel(inputs, *refs):
    sums, middle = take(refs[:inputs])
    put(sums, middle, refs[inputs:])


def add(parts, blocks):
    count, width = parts[0].shape
    shape = [jax.ShapeDtypeStruct((count // blocks, width), BF16)] * blocks
    kernel = functools.partial(add_kernel, len(parts))
    return call(kernel, shape, [WHOLE] * len(parts), 0.2, "add", limit=4 * MIB)(*parts)


def low_rank(x, w_in, w_out):
    low = lax.dot_general(x, w_in[...], (((1,), (1,)), ((), ())), preferred_element_type=F32)
    return 0.5 * jnp.dot(low.astype(BF16), w_out[...], preferred_element_type=F32)


def layer_kernel(
    rows, gate, up, down, gate_in, gate_out, up_in, up_out, down_in, keep, send, gate_low, up_low, hidden, held, arrived
):
    width, out_width = gate.shape[1], down.shape[1]
    piece = out_width // PIECES
    copies = []
    for i in range(PIECES):
        part = pl.ds(i * piece, piece)
        copies.append(pltpu.make_async_copy(down.at[:, part], held.at[:, part], arrived.at[i]))
    for copy in copies:
        copy.start()
    x = rows[...]
    gate_low[...] = low_rank(x, gate_in, gate_out)
    up_low[...] = low_rank(x, up_in, up_out)
    step = min(512, width)

    @pl.loop(0, width // step)
    def _(j):
        block = pl.ds(pl.multiple_of(j * step, step), step)
        g = jnp.dot(x, gate[:, block], preferred_element_type=F32) + gate_low[:, block]
        u = jnp.dot(x, up[:, block], preferred_element_type=F32) + up_low[:, block]
        hidden[:, block] = (g / (1.0 + jnp.exp(-g)) * u).astype(BF16)

    h = hidden[...]
    count = keep.shape[0]
    middle = lax.dot_general(h, down_in[...], (((1,), (1,)), ((), ())), preferred_element_type=F32)
    high = middle.astype(BF16)
    low = (middle - high.astype(F32)).astype(BF16)
    rank = middle.shape[1]
    for i, target in enumerate((keep, send)):
        part = slice(i * count, (i + 1) * count)
        target[:, out_width:] = jnp.zeros((count, 2 * LANES), BF16)
        target[:, out_width : out_width + rank] = high[part]
        target[:, out_width + LANES : out_width + LANES + rank] = low[part]
    for i, copy in enumerate(copies):
        copy.wait()
        for start in range(i * piece, (i + 1) * piece, 512):
            block = slice(start, start + 512)
            sums = jnp.dot(h, held[:, block], preferred_element_type=F32).astype(BF16)
            keep[:, block] = sums[:count]
            send[:, block] = sums[count:]


def last_kernel(mine, theirs, down_out, mixed, importance):
    sums, middle = take((mine, theirs))
    count, rank = mine.shape[0], down_out.shape[0]
    rest = middle[:, :rank]
    adapter = jnp.zeros(sums.shape, F32)
    for _ in range(3):
        part = rest.astype(BF16)
        rest = rest - part.astype(F32)
        adapter += jnp.dot(part, down_out[...], preferred_element_type=F32)
    adapter = 0.5 * adapter
    mixed[...] = (sums + adapter).astype(BF16)
    norm = jnp.sqrt(jnp.sum(adapter * adapter, axis=1, keepdims=True))
    row = lax.broadcasted_iota(jnp.int32, (count, count), 0)
    column = lax.broadcasted_iota(jnp.int32, (count, count), 1)
    importance[...] = jnp.sum(jnp.where(row == column, norm, 0.0), axis=0, keepdims=True)


def body(size, along_x, tokens, gate, up, down, gate_in, gate_out, up_in, up_out, down_in, down_out):
    rounds = rounds_of(size, along_x)
    width, out_width = gate.shape[1], down.shape[1]
    held = call(hold_kernel, jax.ShapeDtypeStruct(tokens.shape, tokens.dtype), [FAR], HOLD_US, "hold")(hbm(tokens))
    rows = tokens
    for k, masks in enumerate(rounds):
        theirs = [swap(rows, size, mask) for mask in masks]
        rows = merge([held if k == 0 else rows] + theirs, MERGE_US[min(k, len(MERGE_US) - 1)])
    count = rows.shape[0]
    parts = call(
        layer_kernel,
        [jax.ShapeDtypeStruct((count // 2, out_width + 2 * LANES), BF16)] * 2,
        [WHOLE] * 3 + [FAR] + [WHOLE] * 5,
        9,
        "layer",
        limit=down.size * 2 + (2 + count // 64 * 2) * MIB,
        scratch=[
            pltpu.VMEM((count, width), F32),
            pltpu.VMEM((count, width), F32),
            pltpu.VMEM((count, width), BF16),
            pltpu.VMEM(down.shape, BF16),
            pltpu.SemaphoreType.DMA((PIECES,)),
        ],
    )(rows, vmem(gate), vmem(up), hbm(down), gate_in.T, gate_out, up_in.T, up_out, down_in.T)
    for masks, after in zip(rounds[::-1], rounds[-2::-1]):
        theirs = [swap(part, size, mask) for part, mask in zip(parts[1:], masks)]
        parts = add([parts[0]] + theirs, 1 + len(after))
    theirs = swap(parts[1], size, rounds[0][0])
    mixed, importance = call(
        last_kernel,
        [jax.ShapeDtypeStruct(tokens.shape, BF16), jax.ShapeDtypeStruct((1, tokens.shape[0]), F32)],
        [WHOLE] * 3,
        1,
        "last",
        limit=4 * MIB,
    )(parts[0], theirs, down_out)
    return mixed, importance.reshape(-1)


def solution(mesh):
    size = mesh.shape["blk"]
    along_x = 2 if size <= 16 else 4
    in_specs = (
        P(("grp", "blk"), None),
        P(None, "blk"),
        P(None, "blk"),
        P("blk", None),
        P(),
        P(None, "blk"),
        P(),
        P(None, "blk"),
        P("blk", None),
        P(),
    )
    out_specs = (P(("grp", "blk"), None), P(("grp", "blk")))
    return jax.shard_map(
        functools.partial(body, size, along_x),
        mesh=mesh,
        in_specs=in_specs,
        out_specs=out_specs,
        check_vma=False,
    )
```

```python
import functools

import jax
import jax.numpy as jnp
from jax import lax
from jax.experimental import pallas as pl
from jax.experimental.pallas import tpu as pltpu
from jax.sharding import PartitionSpec as P

MIB = 1 << 20
LANES = 128
FLOPS_PER_US = 10**9
HOLD_US, MERGE_US = 2, (2, 4, 2)
F32, BF16 = jnp.float32, jnp.bfloat16
WHOLE = pl.BlockSpec(memory_space=pltpu.VMEM)
FAR = pl.BlockSpec(memory_space=pltpu.HBM)
vmem = functools.partial(pltpu.with_memory_space_constraint, memory_space=pltpu.VMEM)
hbm = functools.partial(pltpu.with_memory_space_constraint, memory_space=pltpu.HBM)


def call(kernel, out_shape, in_specs, us, name, limit=2 * MIB, scratch=()):
    many = isinstance(out_shape, list)
    return pl.pallas_call(
        kernel,
        out_shape=out_shape,
        in_specs=in_specs,
        out_specs=[WHOLE] * len(out_shape) if many else WHOLE,
        scratch_shapes=list(scratch),
        compiler_params=pltpu.CompilerParams(vmem_limit_bytes=limit),
        cost_estimate=pl.CostEstimate(flops=int(us * FLOPS_PER_US), bytes_accessed=0, transcendentals=0),
        name=name,
    )


def rounds_of(size, along_x):
    masks = [1 << b for b in range(size.bit_length() - 1)]
    x, z = 2, 2 * along_x
    return [[m] for m in reversed(masks) if m not in (1, x, z)] + [[x, z, x ^ z], [1]]


def swap(value, size, mask):
    return lax.ppermute(value, "blk", [(i, i ^ mask) for i in range(size)])


def hold_kernel(source, target):
    pltpu.sync_copy(source, target)


def merge_kernel(*refs):
    merged = refs[-1]
    count = refs[0].shape[0]
    for i, part in enumerate(refs[:-1]):
        merged[i * count : (i + 1) * count] = part[...]


def merge(parts, us):
    count, width = parts[0].shape
    shape = jax.ShapeDtypeStruct((len(parts) * count, width), parts[0].dtype)
    return call(merge_kernel, shape, [WHOLE] * len(parts), us, "merge")(*parts)


def put(sums, middle, targets):
    high = middle.astype(BF16)
    low = (middle - high.astype(F32)).astype(BF16)
    width, rank = sums.shape[1], middle.shape[1]
    count = targets[0].shape[0]
    for i, target in enumerate(targets):
        rows = slice(i * count, (i + 1) * count)
        target[:, :width] = sums[rows].astype(BF16)
        target[:, width : width + rank] = high[rows]
        target[:, width + LANES : width + LANES + rank] = low[rows]


def take(parts):
    width = parts[0].shape[1] - 2 * LANES
    sums = sum(part[:, :width].astype(F32) for part in parts)
    middle = sum(part[:, width : width + LANES].astype(F32) + part[:, width + LANES :].astype(F32) for part in parts)
    return sums, middle


def add_kernel(inputs, *refs):
    sums, middle = take(refs[:inputs])
    put(sums, middle, refs[inputs:])


def add(parts, blocks):
    count, width = parts[0].shape
    shape = [jax.ShapeDtypeStruct((count // blocks, width), BF16)] * blocks
    kernel = functools.partial(add_kernel, len(parts))
    return call(kernel, shape, [WHOLE] * len(parts), 0.2, "add", limit=4 * MIB)(*parts)


def layer_kernel(
    rows, gate, up, down, gate_in, gate_out, up_in, up_out, down_in, keep, send,
    maps, gate_low, up_low, hidden, held, arrived,
):
    width, out_width = gate.shape[1], down.shape[1]
    copy = pltpu.make_async_copy(down, held, arrived)
    copy.start()
    x = rows[...]
    across = (((1,), (1,)), ((), ()))
    rank = gate_in.shape[0]
    maps[:rank] = gate_in[...]
    maps[rank:] = up_in[...]
    low = lax.dot_general(x, maps[...], across, preferred_element_type=F32).astype(BF16)
    gate_low[...] = 0.5 * jnp.dot(low[:, :rank], gate_out[...], preferred_element_type=F32)
    up_low[...] = 0.5 * jnp.dot(low[:, rank:], up_out[...], preferred_element_type=F32)
    step = min(512, width)

    @pl.loop(0, width // step)
    def _(j):
        block = pl.ds(pl.multiple_of(j * step, step), step)
        g = jnp.dot(x, gate[:, block], preferred_element_type=F32) + gate_low[:, block]
        u = jnp.dot(x, up[:, block], preferred_element_type=F32) + up_low[:, block]
        hidden[:, block] = (g / (1.0 + jnp.exp(-g)) * u).astype(BF16)

    h = hidden[...]
    count = keep.shape[0]
    middle = lax.dot_general(h, down_in[...], across, preferred_element_type=F32)
    high = middle.astype(BF16)
    low = (middle - high.astype(F32)).astype(BF16)
    for i, target in enumerate((keep, send)):
        part = slice(i * count, (i + 1) * count)
        target[:, out_width:] = jnp.zeros((count, 2 * LANES), BF16)
        target[:, out_width : out_width + rank] = high[part]
        target[:, out_width + LANES : out_width + LANES + rank] = low[part]
    copy.wait()
    for start in range(0, out_width, 1024):
        block = slice(start, start + 1024)
        sums = jnp.dot(h, held[:, block], preferred_element_type=F32).astype(BF16)
        keep[:, block] = sums[:count]
        send[:, block] = sums[count:]


def last_kernel(mine, theirs, down_out, mixed, importance):
    sums, middle = take((mine, theirs))
    count, rank = mine.shape[0], down_out.shape[0]
    rest, parts = middle[:, :rank], []
    for _ in range(3):
        parts.append(rest.astype(BF16))
        rest = rest - parts[-1].astype(F32)
    product = jnp.dot(jnp.concatenate(parts, axis=0), down_out[...], preferred_element_type=F32)
    adapter = 0.5 * (product[:count] + product[count : 2 * count] + product[2 * count :])
    mixed[...] = (sums + adapter).astype(BF16)
    norm = jnp.sqrt(jnp.sum(adapter * adapter, axis=1, keepdims=True))
    row = lax.broadcasted_iota(jnp.int32, (count, count), 0)
    column = lax.broadcasted_iota(jnp.int32, (count, count), 1)
    importance[...] = jnp.sum(jnp.where(row == column, norm, 0.0), axis=0, keepdims=True)


def body(size, along_x, tokens, gate, up, down, gate_in, gate_out, up_in, up_out, down_in, down_out):
    rounds = rounds_of(size, along_x)
    width, out_width = gate.shape[1], down.shape[1]
    held = call(hold_kernel, jax.ShapeDtypeStruct(tokens.shape, tokens.dtype), [FAR], HOLD_US, "hold")(hbm(tokens))
    rows = tokens
    for k, masks in enumerate(rounds):
        theirs = [swap(rows, size, mask) for mask in masks]
        rows = merge([held if k == 0 else rows] + theirs, MERGE_US[min(k, len(MERGE_US) - 1)])
    count = rows.shape[0]
    parts = call(
        layer_kernel,
        [jax.ShapeDtypeStruct((count // 2, out_width + 2 * LANES), BF16)] * 2,
        [WHOLE] * 3 + [FAR] + [WHOLE] * 5,
        9,
        "layer",
        limit=down.size * 2 + (2 + count // 64 * 2) * MIB,
        scratch=[
            pltpu.VMEM((2 * gate_in.shape[1], gate_in.shape[0]), BF16),
            pltpu.VMEM((count, width), F32),
            pltpu.VMEM((count, width), F32),
            pltpu.VMEM((count, width), BF16),
            pltpu.VMEM(down.shape, BF16),
            pltpu.SemaphoreType.DMA(()),
        ],
    )(rows, vmem(gate), vmem(up), hbm(down), gate_in.T, gate_out, up_in.T, up_out, down_in.T)
    for masks, after in zip(rounds[::-1], rounds[-2::-1]):
        theirs = [swap(part, size, mask) for part, mask in zip(parts[1:], masks)]
        parts = add([parts[0]] + theirs, 1 + len(after))
    theirs = swap(parts[1], size, rounds[0][0])
    mixed, importance = call(
        last_kernel,
        [jax.ShapeDtypeStruct(tokens.shape, BF16), jax.ShapeDtypeStruct((1, tokens.shape[0]), F32)],
        [WHOLE] * 3,
        1,
        "last",
        limit=4 * MIB,
    )(parts[0], theirs, down_out)
    return mixed, importance.reshape(-1)


def solution(mesh):
    size = mesh.shape["blk"]
    along_x = 2 if size <= 16 else 4
    in_specs = (
        P(("grp", "blk"), None),
        P(None, "blk"),
        P(None, "blk"),
        P("blk", None),
        P(),
        P(None, "blk"),
        P(),
        P(None, "blk"),
        P("blk", None),
        P(),
    )
    out_specs = (P(("grp", "blk"), None), P(("grp", "blk")))
    return jax.shard_map(
        functools.partial(body, size, along_x),
        mesh=mesh,
        in_specs=in_specs,
        out_specs=out_specs,
        check_vma=False,
    )
```

```python
import functools

import jax
import jax.numpy as jnp
from jax import lax
from jax.experimental import pallas as pl
from jax.experimental.pallas import tpu as pltpu
from jax.sharding import PartitionSpec as P

MIB = 1 << 20
LANES = 128
FLOPS_PER_US = 10**9
HOLD_US, MERGE_US = 3, (2, 5)
F32, BF16 = jnp.float32, jnp.bfloat16
WHOLE = pl.BlockSpec(memory_space=pltpu.VMEM)
FAR = pl.BlockSpec(memory_space=pltpu.HBM)
vmem = functools.partial(pltpu.with_memory_space_constraint, memory_space=pltpu.VMEM)
hbm = functools.partial(pltpu.with_memory_space_constraint, memory_space=pltpu.HBM)


def call(kernel, out_shape, in_specs, us, name, limit=2 * MIB, scratch=()):
    many = isinstance(out_shape, list)
    return pl.pallas_call(
        kernel,
        out_shape=out_shape,
        in_specs=in_specs,
        out_specs=[WHOLE] * len(out_shape) if many else WHOLE,
        scratch_shapes=list(scratch),
        compiler_params=pltpu.CompilerParams(vmem_limit_bytes=limit),
        cost_estimate=pl.CostEstimate(flops=int(us * FLOPS_PER_US), bytes_accessed=0, transcendentals=0),
        name=name,
    )


def rounds_of(size, along_x):
    masks = [1 << b for b in range(size.bit_length() - 1)]
    x, z = 2, 2 * along_x
    return [[m] for m in reversed(masks) if m not in (1, x, z)] + [[x ^ z, z, x], [1]]


def swap(value, size, mask):
    return lax.ppermute(value, "blk", [(i, i ^ mask) for i in range(size)])


def hold_kernel(source, target):
    pltpu.sync_copy(source, target)


def merge_kernel(*refs):
    merged = refs[-1]
    count = refs[0].shape[0]
    for i, part in enumerate(refs[:-1]):
        merged[i * count : (i + 1) * count] = part[...]


def merge(parts, us):
    count, width = parts[0].shape
    shape = jax.ShapeDtypeStruct((len(parts) * count, width), parts[0].dtype)
    return call(merge_kernel, shape, [WHOLE] * len(parts), us, "merge")(*parts)


def put(sums, middle, targets):
    high = middle.astype(BF16)
    low = (middle - high.astype(F32)).astype(BF16)
    width, rank = sums.shape[1], middle.shape[1]
    count = targets[0].shape[0]
    for i, target in enumerate(targets):
        rows = slice(i * count, (i + 1) * count)
        target[:, :width] = sums[rows].astype(BF16)
        target[:, width : width + rank] = high[rows]
        target[:, width + LANES : width + LANES + rank] = low[rows]


def take(parts):
    width = parts[0].shape[1] - 2 * LANES
    sums = sum(part[:, :width].astype(F32) for part in parts)
    middle = sum(part[:, width : width + LANES].astype(F32) + part[:, width + LANES :].astype(F32) for part in parts)
    return sums, middle


def add_kernel(inputs, *refs):
    sums, middle = take(refs[:inputs])
    put(sums, middle, refs[inputs:])


def add(parts, blocks):
    count, width = parts[0].shape
    shape = [jax.ShapeDtypeStruct((count // blocks, width), BF16)] * blocks
    kernel = functools.partial(add_kernel, len(parts))
    return call(kernel, shape, [WHOLE] * len(parts), 0.2, "add", limit=4 * MIB)(*parts)


def layer_kernel(
    mine_a, mine_b, theirs_a, theirs_b, gate, up, down, gate_in, gate_out, up_in, up_out, down_in, keep, send,
    maps, gate_low, up_low, hidden, held, arrived,
):
    width, out_width = gate.shape[1], down.shape[1]
    copy = pltpu.make_async_copy(down, held, arrived)
    copy.start()
    x = jnp.concatenate([mine_a[...], mine_b[...], theirs_a[...], theirs_b[...]], axis=0)
    across = (((1,), (1,)), ((), ()))
    rank = gate_in.shape[0]
    maps[:rank] = gate_in[...]
    maps[rank:] = up_in[...]
    low = lax.dot_general(x, maps[...], across, preferred_element_type=F32).astype(BF16)
    gate_low[...] = 0.5 * jnp.dot(low[:, :rank], gate_out[...], preferred_element_type=F32)
    up_low[...] = 0.5 * jnp.dot(low[:, rank:], up_out[...], preferred_element_type=F32)
    step = min(512, width)

    @pl.loop(0, width // step)
    def _(j):
        block = pl.ds(pl.multiple_of(j * step, step), step)
        g = jnp.dot(x, gate[:, block], preferred_element_type=F32) + gate_low[:, block]
        u = jnp.dot(x, up[:, block], preferred_element_type=F32) + up_low[:, block]
        hidden[:, block] = (g / (1.0 + jnp.exp(-g)) * u).astype(BF16)

    h = hidden[...]
    count = keep.shape[0]
    middle = lax.dot_general(h, down_in[...], across, preferred_element_type=F32)
    high = middle.astype(BF16)
    low = (middle - high.astype(F32)).astype(BF16)
    for i, target in enumerate((keep, send)):
        part = slice(i * count, (i + 1) * count)
        target[:, out_width:] = jnp.zeros((count, 2 * LANES), BF16)
        target[:, out_width : out_width + rank] = high[part]
        target[:, out_width + LANES : out_width + LANES + rank] = low[part]
    copy.wait()
    for start in range(0, out_width, 1024):
        block = slice(start, start + 1024)
        sums = jnp.dot(h, held[:, block], preferred_element_type=F32).astype(BF16)
        keep[:, block] = sums[:count]
        send[:, block] = sums[count:]


def last_kernel(mine, theirs, down_out, mixed, importance):
    sums, middle = take((mine, theirs))
    count, rank = mine.shape[0], down_out.shape[0]
    rest, parts = middle[:, :rank], []
    for _ in range(3):
        parts.append(rest.astype(BF16))
        rest = rest - parts[-1].astype(F32)
    product = jnp.dot(jnp.concatenate(parts, axis=0), down_out[...], preferred_element_type=F32)
    adapter = 0.5 * (product[:count] + product[count : 2 * count] + product[2 * count :])
    mixed[...] = (sums + adapter).astype(BF16)
    norm = jnp.sqrt(jnp.sum(adapter * adapter, axis=1, keepdims=True))
    row = lax.broadcasted_iota(jnp.int32, (count, count), 0)
    column = lax.broadcasted_iota(jnp.int32, (count, count), 1)
    importance[...] = jnp.sum(jnp.where(row == column, norm, 0.0), axis=0, keepdims=True)


def body(size, along_x, tokens, gate, up, down, gate_in, gate_out, up_in, up_out, down_in, down_out):
    rounds = rounds_of(size, along_x)
    width, out_width = gate.shape[1], down.shape[1]
    held = call(hold_kernel, jax.ShapeDtypeStruct(tokens.shape, tokens.dtype), [FAR], HOLD_US, "hold")(hbm(tokens))
    rows = tokens
    for k, masks in enumerate(rounds[:-2]):
        rows = merge([held if k == 0 else rows, swap(rows, size, masks[0])], MERGE_US[0])
    far, near, last = [swap(rows, size, mask) for mask in rounds[-2]]
    mine = [merge([rows, far], 1), merge([near, last], MERGE_US[1])]
    theirs = [swap(part, size, 1) for part in mine]
    count = 8 * rows.shape[0]
    parts = call(
        layer_kernel,
        [jax.ShapeDtypeStruct((count // 2, out_width + 2 * LANES), BF16)] * 2,
        [WHOLE] * 6 + [FAR] + [WHOLE] * 5,
        9,
        "layer",
        limit=down.size * 2 + (2 + count // 64 * 2) * MIB,
        scratch=[
            pltpu.VMEM((2 * gate_in.shape[1], gate_in.shape[0]), BF16),
            pltpu.VMEM((count, width), F32),
            pltpu.VMEM((count, width), F32),
            pltpu.VMEM((count, width), BF16),
            pltpu.VMEM(down.shape, BF16),
            pltpu.SemaphoreType.DMA(()),
        ],
    )(*mine, *theirs, vmem(gate), vmem(up), hbm(down), gate_in.T, gate_out, up_in.T, up_out, down_in.T)
    for masks, after in zip(rounds[::-1], rounds[-2::-1]):
        theirs = [swap(part, size, mask) for part, mask in zip(parts[1:], masks)]
        parts = add([parts[0]] + theirs, 1 + len(after))
    theirs = swap(parts[1], size, rounds[0][0])
    mixed, importance = call(
        last_kernel,
        [jax.ShapeDtypeStruct(tokens.shape, BF16), jax.ShapeDtypeStruct((1, tokens.shape[0]), F32)],
        [WHOLE] * 3,
        1,
        "last",
        limit=4 * MIB,
    )(parts[0], theirs, down_out)
    return mixed, importance.reshape(-1)


def solution(mesh):
    size = mesh.shape["blk"]
    along_x = 2 if size <= 16 else 4
    in_specs = (
        P(("grp", "blk"), None),
        P(None, "blk"),
        P(None, "blk"),
        P("blk", None),
        P(),
        P(None, "blk"),
        P(),
        P(None, "blk"),
        P("blk", None),
        P(),
    )
    out_specs = (P(("grp", "blk"), None), P(("grp", "blk")))
    return jax.shard_map(
        functools.partial(body, size, along_x),
        mesh=mesh,
        in_specs=in_specs,
        out_specs=out_specs,
        check_vma=False,
    )
```
